32 devices in a mesh: dp: 16 (over z, x, core), shard: 2 (over y).
Axes of the slice: x: 2, y: 2, z: 4, core: 2. Of those that a mesh axis runs over, the one named last changes fastest.
Arguments:
- clips: bfloat16 [64, 5, 256, 512], P(('dp', 'shard')), may hold values from -16 to 16
- code_grad: bfloat16 [64, 5, 256, 18], P(('dp', 'shard')), may hold values from -6 to 6
- conv_weight: bfloat16 [1536, 512], replicated, may hold values from -0.15625 to 0.15625
- norm_gain: float32 [512], replicated, may hold values from 0.5 to 1.5
- proj_weight: bfloat16 [512, 18], replicated, may hold values from -0.25 to 0.25
- code_bias: float32 [18], replicated, may hold values from -1 to 1
- rotation: float32 [18, 18], replicated, may hold values from -1.5 to 1.5
- first_moment: float32 [1536, 512], P('shard'), may hold values from -4 to 4
- second_moment: float32 [1536, 512], P('shard'), may hold values from 0.01 to 0.3
Outputs:
- new_weight: bfloat16 [1536, 512], replicated
- first_moment_out: float32 [1536, 512], P('shard')
- second_moment_out: float32 [1536, 512], P('shard')
- input_grad: bfloat16 [64, 5, 256, 512], P(('dp', 'shard'))
- loss: float32 [], replicated
The draws below stay inside these ranges and needn't reach their ends.
All inputs are finite; a program needn't handle non-finite values.
Results may differ from the reference program's by a relative error of at most 0.014.
Values may be sent and summed in bfloat16 or wider, within the bound.
A program may use at most 128 MiB of HBM per device.

```python
import math
import jax
import jax.numpy as jnp
from jax import lax

C = 512
BITS = 18
FRAMES = 5
SITES = 256
CLIP_DEV = 2
CLIPS = 64


def draw_clips(key, part):
    block_count = CLIPS // CLIP_DEV
    jitter_key = jax.random.fold_in(key, 11)
    offset_key = jax.random.fold_in(key, 23)
    spike_key = jax.random.fold_in(key, 37)
    extent = (CLIPS, FRAMES, SITES, C)
    jitter = jnp.clip(jax.random.normal(jitter_key, extent, jnp.float32), -4.0, 4.0)
    offset = jnp.clip(1.5 * jax.random.normal(offset_key, (block_count, C), jnp.float32), -4.5, 4.5)
    chosen = jax.random.randint(spike_key, (block_count, 1), 0, C)
    factor = jnp.where(jnp.arange(C)[None, :] == chosen, 4.0, 1.0).astype(jnp.float32)
    offset = jnp.repeat(offset, CLIP_DEV, axis=0)
    factor = jnp.repeat(factor, CLIP_DEV, axis=0)
    values = jitter * factor[:, None, None, :] + offset[:, None, None, :]
    return jnp.clip(values, -16.0, 16.0).astype(jnp.bfloat16)


def steps_of(own_key, dims, cuts, smallest, high):
    def one(dim, blocks):
        steps = jax.random.uniform(jax.random.fold_in(jax.random.fold_in(own_key, 6), dim), (blocks,), jnp.float32, smallest / len(cuts), high / len(cuts))
        return jnp.repeat(jnp.exp(steps), dims[dim] // blocks).reshape((-1,) + (1,) * (len(dims) - dim - 1))

    level = one(*cuts[0])
    for cut in cuts[1:]:
        level = level * one(*cut)
    return level


def bell_draw(rng, shape, spread, reach, shards=(), dtype=jnp.bfloat16):
    factor_of = steps_of(rng, shape, shards, -0.22, 0.18) if shards else 1.0
    drawn = jax.random.normal(rng, shape, jnp.float32) * spread * factor_of
    return jnp.minimum(jnp.maximum(drawn, -reach), reach).astype(dtype)


def setup_inputs(seed: int = 0) -> dict:
    seeds = jax.random.split(jax.random.key(seed), 10)
    return {
        "clips": draw_clips(jax.random.fold_in(seeds[9], 71), 0),
        "code_grad": bell_draw(seeds[1], (CLIPS, FRAMES, SITES, BITS), 1.0, 6.0, ((0, 32),)),
        "conv_weight": bell_draw(seeds[2], (3 * C, C), (3 * C) ** -0.5, 0.15625),
        "norm_gain": jnp.clip(1.0 + 0.1 * jax.random.normal(seeds[3], (C,), jnp.float32), 0.5, 1.5),
        "proj_weight": bell_draw(seeds[4], (C, BITS), C ** -0.5, 0.25),
        "code_bias": jnp.clip(jax.random.uniform(seeds[5], (BITS,), jnp.float32, -1.0, 1.0), -1.0, 1.0),
        "rotation": bell_draw(seeds[6], (BITS, BITS), BITS ** -0.5, 1.5, (), jnp.float32),
        "first_moment": bell_draw(seeds[7], (3 * C, C), 0.3, 4.0, ((0, 2),), jnp.float32),
        "second_moment": jnp.clip(jnp.exp(math.log(0.3) - 3.4011974 * jax.random.uniform(seeds[8], (3 * C, C), jnp.float32) ** steps_of(seeds[8], (3 * C, C), ((0, 2),), -0.2, 0.2)), 0.01, 0.3),
    }


def stacked_taps(block):
    batch, frames, sites, width = block.shape
    padded = jnp.pad(block, ((0, 0), (2, 0), (0, 0), (0, 0)))
    taps = [padded[:, 2 - k:2 - k + frames] for k in range(3)]
    return jnp.concatenate(taps, axis=3).reshape(batch * frames * sites, 3 * width)

def forward(block, conv_weight, norm_gain, proj_weight, code_bias, rotation):
    width = block.shape[3]
    stacked = stacked_taps(block)
    hidden = block.reshape(-1, width).astype(jnp.float32) + jnp.dot(stacked, conv_weight, preferred_element_type=jnp.float32)
    inverse = lax.rsqrt(lax.optimization_barrier(jnp.mean(hidden * hidden, axis=1, keepdims=True)) + 1e-06)
    unit = hidden * inverse
    normed = (unit * norm_gain).astype(jnp.bfloat16)
    latent = jnp.dot(normed, proj_weight, preferred_element_type=jnp.float32) + code_bias
    rotated = jnp.dot(latent, rotation, precision=lax.Precision.HIGHEST)
    codes = jnp.tanh(rotated)
    return (stacked, inverse, unit, rotated, codes)

def token_terms(rotated, codes, cotangent):
    probs = (1.0 + codes) / 2.0
    logit = 2.0 * rotated
    entropy = jax.nn.softplus(logit) - logit * probs
    token_loss = cotangent * codes + 0.25 * (rotated - codes) ** 2 + 0.1 * entropy
    return (probs, logit, jnp.sum(token_loss))

def backward(block, cotangent, conv_weight, norm_gain, proj_weight, rotation, saved, lean, clip_count):
    stacked, inverse, unit, rotated, codes = saved
    probs = (1.0 + codes) / 2.0
    logit = 2.0 * rotated
    slope = 1.0 - codes * codes
    d_rot = (cotangent * slope + 0.5 * (rotated - codes) * (1.0 - slope) - 0.2 * logit * probs * (1.0 - probs) - 0.05 * slope * lean) / clip_count
    d_lat = jnp.dot(d_rot, rotation.T, precision=lax.Precision.HIGHEST)
    d_norm = jnp.dot(d_lat, proj_weight.astype(jnp.float32).T, precision=lax.Precision.HIGHEST)
    scaled = d_norm * norm_gain
    d_hidden = inverse * (scaled - unit * lax.optimization_barrier(jnp.mean(scaled * unit, axis=1, keepdims=True)))
    d_conv = d_hidden.astype(jnp.bfloat16)
    batch, frames, sites, width = block.shape
    d_taps = lax.dot_general(d_conv, conv_weight, (((1,), (1,)), ((), ())), preferred_element_type=jnp.float32)
    d_taps = d_taps.reshape(batch, frames, sites, 3, width)
    padded = jnp.pad(d_taps, ((0, 0), (0, 2), (0, 0), (0, 0), (0, 0)))
    back = padded[:, 0:frames, :, 0, :] + padded[:, 1:frames + 1, :, 1, :] + padded[:, 2:frames + 2, :, 2, :]
    input_grad = (d_hidden.reshape(batch, frames, sites, width) + back).astype(jnp.bfloat16)
    return (stacked, d_conv, input_grad)

def reference(clips, code_grad, conv_weight, norm_gain, proj_weight, code_bias, rotation, first_moment, second_moment):
    clip_count = clips.shape[0]
    token_count = clips.shape[0] * clips.shape[1] * clips.shape[2]
    bit_count = code_grad.shape[3]

    def stats_step(carry, item):
        block, cotangent = item
        saved = forward(block[None], conv_weight, norm_gain, proj_weight, code_bias, rotation)
        probs, logit, loss_part = token_terms(saved[3], saved[4], cotangent.reshape(-1, bit_count).astype(jnp.float32))
        return ((carry[0] + lax.optimization_barrier(jnp.sum(probs, axis=0)), carry[1] + loss_part), None)
    init = (jnp.zeros((bit_count,), jnp.float32), jnp.zeros((), jnp.float32))
    (bit_total, loss_total), _ = lax.scan(stats_step, init, (clips, code_grad))
    bit_mean = bit_total / token_count
    code_entropy = jnp.sum(-bit_mean * jnp.log(bit_mean) - (1.0 - bit_mean) * jnp.log(1.0 - bit_mean))
    loss = loss_total / token_count - 0.1 * code_entropy
    lean = jnp.log((1.0 - bit_mean) / bit_mean)

    def grad_step(carry, item):
        block, cotangent = item
        saved = forward(block[None], conv_weight, norm_gain, proj_weight, code_bias, rotation)
        stacked, d_conv, input_grad = backward(block[None], cotangent.reshape(-1, bit_count).astype(jnp.float32), conv_weight, norm_gain, proj_weight, rotation, saved, lean, clip_count)
        term = lax.dot_general(stacked, d_conv, (((0,), (0,)), ((), ())), preferred_element_type=jnp.float32)
        return (carry + term, input_grad[0])
    grad, input_grad = lax.scan(grad_step, jnp.zeros(conv_weight.shape, jnp.float32), (clips, code_grad))
    first_out = 0.9 * first_moment + 0.1 * grad
    second_out = 0.99 * second_moment + 0.01 * grad * grad
    new_weight = (conv_weight.astype(jnp.float32) - 0.001 * first_out / (jnp.sqrt(second_out) + 1e-08)).astype(jnp.bfloat16)
    return (new_weight, first_out, second_out, input_grad, loss)
```

```python
import functools

import jax
import jax.numpy as jnp
from jax import lax
from jax.experimental import pallas as pl
from jax.experimental.pallas import tpu as pltpu
from jax.sharding import PartitionSpec as P

MESH = pl.DeviceIdType.MESH
F32 = jnp.float32
BF16 = jnp.bfloat16
HIGHEST = lax.Precision.HIGHEST
BITS_PAD = 32
PLANE = 8
LINE = 4
DEPTH = 16

IN_W, IN_CG, IN_M1, IN_M2, OUT_W, OUT_M1, OUT_M2, IN_X = range(8)
(
    T_PLANE,
    T_LINE,
    T_CORE,
    T_FIRST,
    T_SECOND,
    T_ROWS,
    T_GATHER,
    T_GRAD_X,
    T_GRAD_CORE,
    T_NEW_Y,
    T_NEW_CORE,
    T_FAR,
) = (0, 8, 12, 14, 16, 17, 21, 25, 26, 28, 30, 32)

NN = (((1,), (0,)), ((), ()))
NT = (((1,), (1,)), ((), ()))


def dot(a, b, dims=NN, precision=None):
    return lax.dot_general(a, b, dims, precision=precision, preferred_element_type=F32)


def flip(bit, change):
    return bit + (1 - 2 * bit) if change else bit


def kernel(
    sizes,
    clips_hbm,
    cg_hbm,
    weight_hbm,
    gain_ref,
    proj_ref,
    bias_ref,
    rot_ref,
    m1_hbm,
    m2_hbm,
    nw_hbm,
    m1o_hbm,
    m2o_hbm,
    ig_hbm,
    loss_ref,
    xs,
    xt,
    w,
    wt,
    cg,
    unit,
    inv,
    rott,
    cgt,
    dl,
    pp,
    dh,
    dc,
    ig,
    m1,
    m2,
    g,
    r1,
    keep,
    s2,
    r2,
    s3,
    r3,
    s4,
    r4,
    far,
    gr,
    nw,
    stat,
    stat2,
    stat3,
    local_sem,
    send_sem,
    recv_sem,
):
    clips, frames, sites, width, bits, dp_size, far_size, tokens_all, clips_all = sizes
    clip_rows = frames * sites
    half = m1.shape[0]
    per_core, per_x = half // 2, half // 4
    own = half // DEPTH
    dp = lax.axis_index("dp")
    s = lax.axis_index("shard")
    c = dp % 2
    h = (dp // 2) % 2
    z = (dp // 4) % 4
    z0, z1 = z % 2, z // 2
    f = dp // DEPTH

    def plane_peer(r):
        return (dp - c - 2 * h + flip(c, r & 1) + 2 * flip(h, r & 2), flip(s, r & 4))

    def line_at(r):
        return flip(z0, r & 1) + 2 * flip(z1, r & 2)

    def line_peer(r):
        return (dp + 4 * (line_at(r) - z), s)

    def far_at(r):
        return (f + r) % far_size

    def far_peer(r):
        return (dp + DEPTH * (far_at(r) - f), s)

    def send(src, dst, index, peer):
        copy = pltpu.make_async_remote_copy(
            src_ref=src,
            dst_ref=dst,
            send_sem=send_sem.at[index],
            recv_sem=recv_sem.at[index],
            device_id=peer,
            device_id_type=MESH,
        )
        copy.start()
        return copy

    w_in = pltpu.make_async_copy(weight_hbm, w, local_sem.at[IN_W])
    w_in.start()
    x_in = []
    for clip in range(clips):
        rows = pl.ds(clip * clip_rows, clip_rows)
        copy = pltpu.make_async_copy(clips_hbm.at[rows], xs.at[rows], local_sem.at[IN_X + clip])
        copy.start()
        x_in.append(copy)
    cg_in = pltpu.make_async_copy(cg_hbm, cg, local_sem.at[IN_CG])
    cg_in.start()
    m1_in = pltpu.make_async_copy(m1_hbm, m1, local_sem.at[IN_M1])
    m1_in.start()
    m2_in = pltpu.make_async_copy(m2_hbm, m2, local_sem.at[IN_M2])
    m2_in.start()

    barrier = pltpu.get_barrier_semaphore()
    peers = [plane_peer(r) for r in range(1, PLANE)]
    peers += [line_peer(r) for r in range(1, LINE)]
    for r in range(1, far_size):
        peers.append(far_peer(r))
    for peer in peers:
        pl.semaphore_signal(barrier, inc=1, device_id=peer, device_id_type=MESH)

    eye_mask = lax.broadcasted_iota(jnp.int32, (BITS_PAD, bits), 0) == lax.broadcasted_iota(
        jnp.int32, (BITS_PAD, bits), 1
    )
    eye = jnp.where(eye_mask, 1.0, 0.0).astype(F32)
    eye16 = eye.astype(BF16)
    proj_t = dot(eye16, proj_ref[...], NT).astype(BF16)
    pp[...] = jnp.zeros_like(pp)
    pp[0:BITS_PAD, :] = proj_t
    pp[BITS_PAD : 2 * BITS_PAD, :] = proj_t
    dl[...] = jnp.zeros_like(dl)
    rot_rows = dot(eye, rot_ref[...], NN, HIGHEST)
    rot = dot(rot_rows, eye, NT, HIGHEST)
    rot_t = dot(eye, rot_rows, NT, HIGHEST)
    bias = jnp.sum(jnp.where(eye_mask, bias_ref[...], 0.0), axis=1, keepdims=True)
    gain = gain_ref[...]

    w_in.wait()
    for copy in x_in:
        copy.wait()
    cg_in.wait()

    def forward(clip, carry):
        base = pl.multiple_of(clip * clip_rows, clip_rows)
        for frame in range(frames):
            here = pl.ds(pl.multiple_of(base + frame * sites, sites), sites)
            taps = min(frame, 2) + 1
            parts = [
                xs[pl.ds(pl.multiple_of(base + (frame - k) * sites, sites), sites), :]
                for k in range(taps)
            ]
            lhs = parts[0] if taps == 1 else jnp.concatenate(parts, axis=1)
            hidden = parts[0].astype(F32) + dot(lhs, w[0 : taps * width, :])
            scale = lax.rsqrt(jnp.mean(hidden * hidden, axis=1, keepdims=True) + 1e-06)
            u = hidden * scale
            unit[here, :] = u
            inv[here, :] = scale
            normed = (u * gain).astype(BF16)
            lat = dot(proj_t, normed, NT) + bias
            rott[:, here] = dot(rot_t, lat, NN, HIGHEST)
            cgt[:, here] = dot(eye16, cg[here, :], NT)
        return carry

    lax.fori_loop(0, clips, forward, 0)

    rotated = rott[...]
    cotangent = cgt[...]
    codes = jnp.tanh(rotated)
    probs = (1.0 + codes) / 2.0
    logit = 2.0 * rotated
    softplus = jnp.maximum(logit, 0.0) + jnp.log(1.0 + jnp.exp(-jnp.abs(logit)))
    entropy = softplus - logit * probs
    token_loss = cotangent * codes + 0.25 * (rotated - codes) ** 2 + 0.1 * entropy
    real = lax.broadcasted_iota(jnp.int32, (BITS_PAD, 1), 0) < bits
    loss_part = jnp.sum(
        jnp.where(real, jnp.sum(token_loss, axis=1, keepdims=True), 0.0), axis=0, keepdims=True
    )
    bit_part = jnp.sum(probs, axis=1, keepdims=True)
    column = jnp.where(real, bit_part, loss_part)
    stat[0] = jnp.broadcast_to(column, stat.shape[1:])

    pl.semaphore_wait(barrier, len(peers))
    sent = [send(stat.at[0], stat.at[r], T_PLANE + r, plane_peer(r)) for r in range(1, PLANE)]

    for k in range(3):
        wt[k * width : (k + 1) * width, :] = w[k * width : (k + 1) * width, :].T
    for copy in sent:
        copy.wait()
    total = stat[0]
    for r in range(1, PLANE):
        total = total + stat[r]
    stat2[0] = total
    sent = [send(stat2.at[0], stat2.at[r], T_LINE + r, line_peer(r)) for r in range(1, LINE)]

    def turn(clip, carry):
        base = pl.multiple_of(clip * clip_rows, clip_rows)
        for frame in range(frames):
            here = pl.ds(pl.multiple_of(base + frame * sites, sites), sites)
            xt[:, here] = xs[here, :].T
        return carry

    lax.fori_loop(0, clips, turn, 0)
    for copy in sent:
        copy.wait()
    total = stat2[0]
    for r in range(1, LINE):
        total = total + stat2[r]
    if far_size > 1:
        stat3[f] = total
        sent = [
            send(stat3.at[f], stat3.at[f], T_FAR + r, far_peer(r)) for r in range(1, far_size)
        ]
        for copy in sent:
            copy.wait()
        total = stat3[0]
        for r in range(1, far_size):
            total = total + stat3[r]
    total = total[:, 0:1]
    bit_mean = jnp.where(real, total / tokens_all, 0.5)
    code_entropy = -bit_mean * jnp.log(bit_mean) - (1.0 - bit_mean) * jnp.log(1.0 - bit_mean)
    code_entropy = jnp.sum(jnp.where(real, code_entropy, 0.0), axis=0, keepdims=True)
    loss_ref[...] = total[bits : bits + 1, :] / tokens_all - 0.1 * code_entropy
    lean = jnp.log((1.0 - bit_mean) / bit_mean)

    rotated = rott[...]
    codes = jnp.tanh(rotated)
    probs = (1.0 + codes) / 2.0
    logit = 2.0 * rotated
    slope = 1.0 - codes * codes
    d_rot = (
        cgt[...] * slope
        + 0.5 * (rotated - codes) * (1.0 - slope)
        - 0.2 * logit * probs * (1.0 - probs)
        - 0.05 * slope * lean
    ) / clips_all
    d_lat = dot(rot, d_rot, NN, HIGHEST)
    high = d_lat.astype(BF16)
    dl[0:BITS_PAD, :] = high.astype(F32)
    dl[BITS_PAD : 2 * BITS_PAD, :] = d_lat - high.astype(F32)

    def back(clip, carry):
        base = pl.multiple_of(clip * clip_rows, clip_rows)
        for frame in range(frames):
            here = pl.ds(pl.multiple_of(base + frame * sites, sites), sites)
            a = dot(dl[:, here].T.astype(BF16), pp[...]) * gain
            u = unit[here, :]
            d_hidden = inv[here, :] * (a - u * jnp.mean(a * u, axis=1, keepdims=True))
            dh[here, :] = d_hidden
            dc[here, :] = d_hidden.astype(BF16)
        return carry

    lax.fori_loop(0, clips, back, 0)

    core_peer = plane_peer(1)
    core_sent = []
    for k in range(3):
        term = None
        for clip in range(clips):
            start = clip * clip_rows
            depth = (frames - k) * sites
            part = dot(
                xt[:, start : start + depth],
                dc[start + k * sites : start + clip_rows, :],
            )
            term = part if term is None else term + part
        g[k * width : (k + 1) * width, :] = term
        for j in range(2):
            if (k + 1) * width >= (j + 1) * half > k * width:
                rows = pl.ds(pl.multiple_of(j * half + (1 - c) * per_core, 8), per_core)
                core_sent.append(send(g.at[rows], r1.at[j], T_CORE + j, core_peer))

    def input_grad(clip):
        base = clip * clip_rows
        for frame in range(frames):
            here = pl.ds(base + frame * sites, sites)
            taps = min(frames - 1 - frame, 2) + 1
            parts = [dc[pl.ds(base + (frame + k) * sites, sites), :] for k in range(taps)]
            lhs = parts[0] if taps == 1 else jnp.concatenate(parts, axis=1)
            ig[here, :] = (dh[here, :] + dot(lhs, wt[0 : taps * width, :])).astype(BF16)
        rows = pl.ds(base, clip_rows)
        copy = pltpu.make_async_copy(ig.at[rows], ig_hbm.at[rows], local_sem.at[IN_X + clips + clip])
        copy.start()
        return copy

    ig_out = []
    for copy in core_sent:
        copy.wait()

    first_peer = (dp + (1 - c) * 2 * (1 - 2 * h), s + c * (1 - 2 * s))
    second_peer = (dp + c * 2 * (1 - 2 * h), s + (1 - c) * (1 - 2 * s))

    def summed(side, x):
        rows = pl.ds(pl.multiple_of(side * half + c * per_core + x * per_x, 8), per_x)
        return g[rows, :] + r1[side, pl.ds(pl.multiple_of(x * per_x, 8), per_x), :]

    first_sent = []
    for j in range(2):
        s2[j] = summed((1 - c) * j + c * (1 - s), (1 - c) * (1 - h) + c * j).astype(BF16)
        first_sent.append(send(s2.at[j], r2.at[j], T_FIRST + j, first_peer))
    for j in range(2):
        keep[j] = summed((1 - c) * j + c * s, (1 - c) * h + c * j)
    ig_out.append(input_grad(0))
    for copy in first_sent:
        copy.wait()
    kept = (1 - c) * s + c * h
    s3[...] = (keep[1 - kept] + r2[1 - kept].astype(F32)).astype(BF16)
    second_sent = send(s3, r3, T_SECOND, second_peer)
    keep[kept] = keep[kept] + r2[kept].astype(F32)
    m1_in.wait()
    m2_in.wait()
    second_sent.wait()
    mine = keep[kept] + r3[...].astype(F32)
    s4[...] = mine.astype(BF16)
    keep[kept] = mine
    rows_sent = []
    for r in range(1, LINE):
        rows = pl.ds(pl.multiple_of(line_at(r) * own, 16), own)
        rows_sent.append(send(s4.at[rows], r4.at[r], T_ROWS + r, line_peer(r)))
    for clip in range(1, clips):
        ig_out.append(input_grad(clip))
    for copy in rows_sent:
        copy.wait()
    grad = keep[kept, pl.ds(pl.multiple_of(z * own, 8), own), :]
    for r in range(1, LINE):
        grad = grad + r4[r].astype(F32)
    if far_size > 1:
        far[f] = grad
        sent = [
            send(far.at[f], far.at[f], T_FAR + far_size + r, far_peer(r))
            for r in range(1, far_size)
        ]
        for copy in sent:
            copy.wait()
        grad = far[0]
        for r in range(1, far_size):
            grad = grad + far[r]

    mine_at = c * per_core + h * per_x
    own_rows = pl.ds(pl.multiple_of(mine_at + z * own, 16), own)
    gr[own_rows, :] = grad.astype(BF16)
    sent = [
        send(gr.at[own_rows], gr.at[own_rows], T_GATHER + r, line_peer(r)) for r in range(1, LINE)
    ]
    for copy in sent:
        copy.wait()

    def update(at):
        rows = pl.ds(pl.multiple_of(at, 16), per_x)
        here = pl.ds(pl.multiple_of(s * half + at, 16), per_x)
        value = gr[rows, :].astype(F32)
        first = 0.9 * m1[rows, :] + 0.1 * value
        second = 0.99 * m2[rows, :] + 0.01 * value * value
        m1[rows, :] = first
        m2[rows, :] = second
        stepped = w[here, :].astype(F32) - 0.001 * first / (jnp.sqrt(second) + 1e-08)
        nw[here, :] = stepped.astype(BF16)

    def grad_rows(at):
        return gr.at[pl.ds(pl.multiple_of(at, 16), per_x)]

    def new_rows(side, at):
        return nw.at[pl.ds(pl.multiple_of(side * half + at, 16), per_x)]

    x_peer, y_peer = plane_peer(2), plane_peer(4)
    other_at = c * per_core + (1 - h) * per_x
    grad_x = send(grad_rows(mine_at), grad_rows(mine_at), T_GRAD_X, x_peer)
    grad_core = [send(grad_rows(mine_at), grad_rows(mine_at), T_GRAD_CORE, core_peer)]
    update(mine_at)
    new_y = [send(new_rows(s, mine_at), new_rows(s, mine_at), T_NEW_Y, y_peer)]
    grad_x.wait()
    grad_core.append(send(grad_rows(other_at), grad_rows(other_at), T_GRAD_CORE + 1, core_peer))
    update(other_at)
    new_y.append(send(new_rows(s, other_at), new_rows(s, other_at), T_NEW_Y + 1, y_peer))
    grad_core[0].wait()
    update((1 - c) * per_core + h * per_x)
    grad_core[1].wait()
    update((1 - c) * per_core + (1 - h) * per_x)
    m1_out = pltpu.make_async_copy(m1, m1o_hbm, local_sem.at[OUT_M1])
    m1_out.start()
    m2_out = pltpu.make_async_copy(m2, m2o_hbm, local_sem.at[OUT_M2])
    m2_out.start()
    new_core = []
    for j, at in enumerate((mine_at, other_at)):
        new_y[j].wait()
        new_core.append(send(new_rows(1 - s, at), new_rows(1 - s, at), T_NEW_CORE + j, core_peer))
    for copy in new_core:
        copy.wait()
    nw_out = pltpu.make_async_copy(nw, nw_hbm, local_sem.at[OUT_W])
    nw_out.start()
    for copy in ig_out:
        copy.wait()
    m1_out.wait()
    m2_out.wait()
    nw_out.wait()


def on_device(
    clips,
    code_grad,
    conv_weight,
    norm_gain,
    proj_weight,
    code_bias,
    rotation,
    first_moment,
    second_moment,
):
    count, frames, sites, width = clips.shape
    bits = code_grad.shape[3]
    dp_size = lax.axis_size("dp")
    devices = dp_size * lax.axis_size("shard")
    far_size = dp_size // DEPTH
    tokens = count * frames * sites
    rows, half = conv_weight.shape[0], first_moment.shape[0]
    per_core, per_x, own = half // 2, half // 4, half // DEPTH
    sizes = (
        count,
        frames,
        sites,
        width,
        bits,
        dp_size,
        far_size,
        tokens * devices,
        count * devices,
    )
    vmem = pltpu.VMEM
    scratch = [
        vmem((tokens, width), BF16),
        vmem((width, tokens), BF16),
        vmem((rows, width), BF16),
        vmem((rows, width), BF16),
        vmem((tokens, bits), BF16),
        vmem((tokens, width), F32),
        vmem((tokens, 1), F32),
        vmem((BITS_PAD, tokens), F32),
        vmem((BITS_PAD, tokens), F32),
        vmem((128, tokens), F32),
        vmem((128, width), BF16),
        vmem((tokens, width), F32),
        vmem((tokens, width), BF16),
        vmem((tokens, width), BF16),
        vmem((half, width), F32),
        vmem((half, width), F32),
        vmem((rows, width), F32),
        vmem((2, per_core, width), F32),
        vmem((2, per_x, width), F32),
        vmem((2, per_x, width), BF16),
        vmem((2, per_x, width), BF16),
        vmem((per_x, width), BF16),
        vmem((per_x, width), BF16),
        vmem((per_x, width), BF16),
        vmem((LINE, own, width), BF16),
        vmem((far_size, own, width), F32),
        vmem((half, width), BF16),
        vmem((rows, width), BF16),
        vmem((PLANE, BITS_PAD, 128), F32),
        vmem((LINE, BITS_PAD, 128), F32),
        vmem((far_size, BITS_PAD, 128), F32),
        pltpu.SemaphoreType.DMA((IN_X + 2 * count,)),
        pltpu.SemaphoreType.DMA((T_FAR + 2 * far_size,)),
        pltpu.SemaphoreType.DMA((T_FAR + 2 * far_size,)),
    ]
    whole = pl.BlockSpec(memory_space=pltpu.VMEM)
    outside = pl.BlockSpec(memory_space=pl.ANY)
    new_weight, first_out, second_out, input_grad, loss = pl.pallas_call(
        functools.partial(kernel, sizes),
        out_shape=(
            jax.ShapeDtypeStruct((rows, width), BF16),
            jax.ShapeDtypeStruct((half, width), F32),
            jax.ShapeDtypeStruct((half, width), F32),
            jax.ShapeDtypeStruct((tokens, width), BF16),
            jax.ShapeDtypeStruct((1, 1), F32),
        ),
        in_specs=[outside, outside, outside, whole, whole, whole, whole, outside, outside],
        out_specs=(outside, outside, outside, outside, whole),
        scratch_shapes=scratch,
        compiler_params=pltpu.CompilerParams(
            collective_id=0, has_side_effects=True, vmem_limit_bytes=60 * 1024 * 1024
        ),
    )(
        clips.reshape(tokens, width),
        code_grad.reshape(tokens, bits),
        conv_weight,
        norm_gain.reshape(1, width),
        proj_weight,
        code_bias.reshape(1, bits),
        rotation,
        first_moment,
        second_moment,
    )
    return (
        new_weight,
        first_out,
        second_out,
        input_grad.reshape(clips.shape),
        loss.reshape(()),
    )


def solution(mesh):
    return jax.shard_map(
        on_device,
        mesh=mesh,
        in_specs=(
            P(("dp", "shard"), None, None, None),
            P(("dp", "shard"), None, None, None),
            P(),
            P(),
            P(),
            P(),
            P(),
            P("shard", None),
            P("shard", None),
        ),
        out_specs=(
            P(),
            P("shard", None),
            P("shard", None),
            P(("dp", "shard"), None, None, None),
            P(),
        ),
        check_vma=False,
    )
```

```python
import functools

import jax
import jax.numpy as jnp
from jax import lax
from jax.experimental import pallas as pl
from jax.experimental.pallas import tpu as pltpu
from jax.sharding import PartitionSpec as P

MESH = pl.DeviceIdType.MESH
F32 = jnp.float32
BF16 = jnp.bfloat16
HIGHEST = lax.Precision.HIGHEST
BITS_PAD = 32
PLANE = 8
LINE = 4
DEPTH = 16
PIECES = 2
VMEM_BYTES = 60 * 1024 * 1024

IN_W, IN_CG, IN_M1, IN_M2, OUT_W, OUT_M1, OUT_M2, IN_X = range(8)
(
    T_PLANE,
    T_LINE,
    T_CORE,
    T_FIRST,
    T_SECOND,
    T_ROWS,
    T_GATHER,
    T_GRAD_X,
    T_GRAD_CORE,
    T_NEW_Y,
    T_NEW_X,
    T_NEW_CORE,
    T_FAR,
) = (0, 8, 12, 14, 16, 17, 21, 25, 29, 37, 45, 47, 55)

NN = (((1,), (0,)), ((), ()))
NT = (((1,), (1,)), ((), ()))


def dot(a, b, dims=NN, precision=None):
    return lax.dot_general(a, b, dims, precision=precision, preferred_element_type=F32)


def flip(bit, change):
    return bit + (1 - 2 * bit) if change else bit


def kernel(
    sizes,
    clips_hbm,
    cg_hbm,
    weight_hbm,
    gain_ref,
    proj_ref,
    bias_ref,
    rot_ref,
    m1_hbm,
    m2_hbm,
    nw_hbm,
    m1o_hbm,
    m2o_hbm,
    ig_hbm,
    loss_ref,
    xs,
    xt,
    w,
    wt,
    cg,
    unit,
    inv,
    lat,
    rott,
    cgt,
    dl,
    pp,
    dc,
    ig,
    m1,
    m2,
    g,
    r1,
    keep,
    s2,
    r2,
    s3,
    r3,
    s4,
    r4,
    far,
    gr,
    nw,
    stat,
    stat2,
    stat3,
    local_sem,
    send_sem,
    recv_sem,
):
    clips, frames, sites, width, bits, dp_size, far_size, tokens_all, clips_all = sizes
    clip_rows = frames * sites
    block = clips * sites
    half = m1.shape[0]
    per_core, per_x = half // 2, half // 4
    own = half // DEPTH
    dp = lax.axis_index("dp")
    s = lax.axis_index("shard")
    c = dp % 2
    h = (dp // 2) % 2
    z = (dp // 4) % 4
    z0, z1 = z % 2, z // 2
    f = dp // DEPTH

    def plane_peer(r):
        return (dp - c - 2 * h + flip(c, r & 1) + 2 * flip(h, r & 2), flip(s, r & 4))

    def line_at(r):
        return flip(z0, r & 1) + 2 * flip(z1, r & 2)

    def line_peer(r):
        return (dp + 4 * (line_at(r) - z), s)

    def far_at(r):
        return (f + r) % far_size

    def far_peer(r):
        return (dp + DEPTH * (far_at(r) - f), s)

    def send(src, dst, index, peer):
        copy = pltpu.make_async_remote_copy(
            src_ref=src,
            dst_ref=dst,
            send_sem=send_sem.at[index],
            recv_sem=recv_sem.at[index],
            device_id=peer,
            device_id_type=MESH,
        )
        copy.start()
        return copy

    w_in = pltpu.make_async_copy(weight_hbm, w, local_sem.at[IN_W])
    w_in.start()
    x_in = []
    for frame in range(frames):
        for clip in range(clips):
            copy = pltpu.make_async_copy(
                clips_hbm.at[pl.ds(clip * clip_rows + frame * sites, sites)],
                xs.at[pl.ds(frame * block + clip * sites, sites)],
                local_sem.at[IN_X + frame * clips + clip],
            )
            copy.start()
            x_in.append(copy)
    cg_in = pltpu.make_async_copy(cg_hbm, cg, local_sem.at[IN_CG])
    cg_in.start()
    m1_in = pltpu.make_async_copy(m1_hbm, m1, local_sem.at[IN_M1])
    m1_in.start()
    m2_in = pltpu.make_async_copy(m2_hbm, m2, local_sem.at[IN_M2])
    m2_in.start()

    barrier = pltpu.get_barrier_semaphore()
    peers = [plane_peer(r) for r in range(1, PLANE)]
    peers += [line_peer(r) for r in range(1, LINE)]
    for r in range(1, far_size):
        peers.append(far_peer(r))
    for peer in peers:
        pl.semaphore_signal(barrier, inc=1, device_id=peer, device_id_type=MESH)

    eye_mask = lax.broadcasted_iota(jnp.int32, (BITS_PAD, bits), 0) == lax.broadcasted_iota(
        jnp.int32, (BITS_PAD, bits), 1
    )
    eye = jnp.where(eye_mask, 1.0, 0.0).astype(F32)
    eye16 = eye.astype(BF16)
    proj_t = dot(eye16, proj_ref[...]).astype(BF16)
    pp[...] = jnp.zeros_like(pp)
    pp[0:BITS_PAD, :] = proj_t
    pp[BITS_PAD : 2 * BITS_PAD, :] = proj_t
    dl[...] = jnp.zeros_like(dl)
    rot_rows = dot(eye, rot_ref[...], NN, HIGHEST)
    rot = dot(rot_rows, eye, NT, HIGHEST)
    rot_t = dot(eye, rot_rows, NT, HIGHEST)
    bias = jnp.sum(jnp.where(eye_mask, bias_ref[...], 0.0), axis=1, keepdims=True)
    gain = gain_ref[...]

    w_in.wait()

    for frame in range(frames):
        here = slice(frame * block, (frame + 1) * block)
        for copy in x_in[frame * clips : (frame + 1) * clips]:
            copy.wait()
        taps = min(frame, 2) + 1
        parts = [xs[(frame - k) * block : (frame - k + 1) * block, :] for k in range(taps)]
        lhs = parts[0] if taps == 1 else jnp.concatenate(parts, axis=1)
        hidden = parts[0].astype(F32) + dot(lhs, w[0 : taps * width, :])
        scale = lax.rsqrt(jnp.mean(hidden * hidden, axis=1, keepdims=True) + 1e-06)
        u = hidden * scale
        unit[here, :] = u
        inv[here, :] = scale
        normed = (u * gain).astype(BF16)
        lat[:, here] = dot(proj_t, normed, NT) + bias

    rott[...] = dot(rot_t, lat[...], NN, HIGHEST)
    cg_in.wait()
    cgt[...] = jnp.zeros_like(cgt)
    for frame in range(frames):
        value = cg[frame].astype(F32)
        for clip in range(clips):
            start = frame * block + clip * sites
            cgt[0:bits, start : start + sites] = value[:, clip, :]
    rotated = rott[...]
    cotangent = cgt[...]
    codes = jnp.tanh(rotated)
    probs = (1.0 + codes) / 2.0
    logit = 2.0 * rotated
    softplus = jnp.maximum(logit, 0.0) + jnp.log(1.0 + jnp.exp(-jnp.abs(logit)))
    entropy = softplus - logit * probs
    token_loss = cotangent * codes + 0.25 * (rotated - codes) ** 2 + 0.1 * entropy
    real = lax.broadcasted_iota(jnp.int32, (BITS_PAD, 1), 0) < bits
    loss_part = jnp.sum(
        jnp.where(real, jnp.sum(token_loss, axis=1, keepdims=True), 0.0), axis=0, keepdims=True
    )
    bit_part = jnp.sum(probs, axis=1, keepdims=True)
    column = jnp.where(real, bit_part, loss_part)
    stat[0] = jnp.broadcast_to(column, stat.shape[1:])

    pl.semaphore_wait(barrier, len(peers))
    sent = [send(stat.at[0], stat.at[r], T_PLANE + r, plane_peer(r)) for r in range(1, PLANE)]

    slope = 1.0 - codes * codes
    base = (
        cotangent * slope
        + 0.5 * (rotated - codes) * (1.0 - slope)
        - 0.2 * logit * probs * (1.0 - probs)
    )
    rott[...] = base / clips_all
    cgt[...] = 0.05 * slope / clips_all
    for k in range(3):
        wt[k * width : (k + 1) * width, :] = w[k * width : (k + 1) * width, :].T
    for copy in sent:
        copy.wait()
    total = stat[0]
    for r in range(1, PLANE):
        total = total + stat[r]
    stat2[0] = total
    sent = [send(stat2.at[0], stat2.at[r], T_LINE + r, line_peer(r)) for r in range(1, LINE)]

    for frame in range(frames):
        here = slice(frame * block, (frame + 1) * block)
        xt[:, here] = xs[here, :].T
    for copy in sent:
        copy.wait()
    total = stat2[0]
    for r in range(1, LINE):
        total = total + stat2[r]
    if far_size > 1:
        stat3[f] = total
        sent = [
            send(stat3.at[f], stat3.at[f], T_FAR + r, far_peer(r)) for r in range(1, far_size)
        ]
        for copy in sent:
            copy.wait()
        total = stat3[0]
        for r in range(1, far_size):
            total = total + stat3[r]
    total = total[:, 0:1]
    bit_mean = jnp.where(real, total / tokens_all, 0.5)
    code_entropy = -bit_mean * jnp.log(bit_mean) - (1.0 - bit_mean) * jnp.log(1.0 - bit_mean)
    code_entropy = jnp.sum(jnp.where(real, code_entropy, 0.0), axis=0, keepdims=True)
    loss_ref[...] = total[bits : bits + 1, :] / tokens_all - 0.1 * code_entropy
    lean = jnp.log((1.0 - bit_mean) / bit_mean)

    d_lat = dot(rot, rott[...] - cgt[...] * lean, NN, HIGHEST)
    high = d_lat.astype(BF16).astype(F32)
    dl[0:BITS_PAD, :] = high
    dl[BITS_PAD : 2 * BITS_PAD, :] = d_lat - high

    for frame in range(frames):
        here = slice(frame * block, (frame + 1) * block)
        a = dot(dl[:, here].T.astype(BF16), pp[...]) * gain
        u = unit[here, :]
        d_hidden = inv[here, :] * (a - u * jnp.mean(a * u, axis=1, keepdims=True))
        dc[here, :] = d_hidden.astype(BF16)

    core_peer = plane_peer(1)
    core_sent = []
    for k in range(3):
        g[k * width : (k + 1) * width, :] = dot(xt[:, 0 : (frames - k) * block], dc[k * block :, :])
        for j in range(2):
            if (k + 1) * width >= (j + 1) * half > k * width:
                rows = pl.ds(pl.multiple_of(j * half + (1 - c) * per_core, 8), per_core)
                core_sent.append(send(g.at[rows], r1.at[j], T_CORE + j, core_peer))

    ig_out = []

    def input_grad(frame):
        here = slice(frame * block, (frame + 1) * block)
        taps = min(frames - 1 - frame, 2) + 1
        parts = [dc[(frame + k) * block : (frame + k + 1) * block, :] for k in range(taps)]
        lhs = parts[0] if taps == 1 else jnp.concatenate(parts, axis=1)
        ig[here, :] = (parts[0].astype(F32) + dot(lhs, wt[0 : taps * width, :])).astype(BF16)
        for clip in range(clips):
            copy = pltpu.make_async_copy(
                ig.at[pl.ds(frame * block + clip * sites, sites)],
                ig_hbm.at[pl.ds(clip * clip_rows + frame * sites, sites)],
                local_sem.at[IN_X + (frames + frame) * clips + clip],
            )
            copy.start()
            ig_out.append(copy)

    input_grad(0)
    for copy in core_sent:
        copy.wait()

    first_peer = (dp + (1 - c) * 2 * (1 - 2 * h), s + c * (1 - 2 * s))
    second_peer = (dp + c * 2 * (1 - 2 * h), s + (1 - c) * (1 - 2 * s))

    def summed(side, x):
        rows = pl.ds(pl.multiple_of(side * half + c * per_core + x * per_x, 8), per_x)
        return g[rows, :] + r1[side, pl.ds(pl.multiple_of(x * per_x, 8), per_x), :]

    kept = (1 - c) * s + c * h
    first_sent = []
    for i, j in enumerate((1 - kept, kept)):
        s2[j] = summed((1 - c) * j + c * (1 - s), (1 - c) * (1 - h) + c * j).astype(BF16)
        first_sent.append(send(s2.at[j], r2.at[j], T_FIRST + i, first_peer))
    for j in range(2):
        keep[j] = summed((1 - c) * j + c * s, (1 - c) * h + c * j)
    input_grad(1)
    first_sent[0].wait()
    s3[...] = (keep[1 - kept] + r2[1 - kept].astype(F32)).astype(BF16)
    second_sent = send(s3, r3, T_SECOND, second_peer)
    input_grad(2)
    m1_in.wait()
    m2_in.wait()
    first_sent[1].wait()
    keep[kept] = keep[kept] + r2[kept].astype(F32)
    second_sent.wait()
    mine = keep[kept] + r3[...].astype(F32)
    s4[...] = mine.astype(BF16)
    keep[kept] = mine
    rows_sent = []
    for r in range(1, LINE):
        rows = pl.ds(pl.multiple_of(line_at(r) * own, 16), own)
        rows_sent.append(send(s4.at[rows], r4.at[r], T_ROWS + r, line_peer(r)))
    for frame in range(3, frames):
        input_grad(frame)
    for copy in rows_sent:
        copy.wait()
    grad = keep[kept, pl.ds(pl.multiple_of(z * own, 8), own), :]
    for r in range(1, LINE):
        grad = grad + r4[r].astype(F32)
    if far_size > 1:
        far[f] = grad
        sent = [
            send(far.at[f], far.at[f], T_FAR + far_size + r, far_peer(r))
            for r in range(1, far_size)
        ]
        for copy in sent:
            copy.wait()
        grad = far[0]
        for r in range(1, far_size):
            grad = grad + far[r]

    def chunk(core, x, r):
        return core * per_core + x * per_x + line_at(r) * own

    def update(at):
        rows = pl.ds(pl.multiple_of(at, 16), own)
        here = pl.ds(pl.multiple_of(s * half + at, 16), own)
        value = gr[rows, :].astype(F32)
        first = 0.9 * m1[rows, :] + 0.1 * value
        second = 0.99 * m2[rows, :] + 0.01 * value * value
        m1[rows, :] = first
        m2[rows, :] = second
        stepped = w[here, :].astype(F32) - 0.001 * first / (jnp.sqrt(second) + 1e-08)
        nw[here, :] = stepped.astype(BF16)

    def send_grad(at, index, peer):
        rows = gr.at[pl.ds(pl.multiple_of(at, 16), own)]
        return send(rows, rows, index, peer)

    def send_new(side, at, index, peer):
        rows = nw.at[pl.ds(pl.multiple_of(side * half + at, 16), own)]
        return send(rows, rows, index, peer)

    x_peer, y_peer = plane_peer(2), plane_peer(4)
    own_at = chunk(c, h, 0)
    gr[pl.ds(pl.multiple_of(own_at, 16), own), :] = grad.astype(BF16)
    gather = [send_grad(own_at, T_GATHER + r, line_peer(r)) for r in range(1, LINE)]
    grad_x, grad_core, new_y, new_x, new_core = [], [], [], [], []
    for r in range(LINE):
        at = chunk(c, h, r)
        if r > 0:
            gather[r - 1].wait()
        grad_x.append(send_grad(at, T_GRAD_X + r, x_peer))
        update(at)
        new_y.append(send_new(s, at, T_NEW_Y + r, y_peer))
        grad_core.append(send_grad(at, T_GRAD_CORE + r, core_peer))
    for r in range(2):
        at = chunk(c, h, r)
        new_y[r].wait()
        new_x.append(send_new(1 - s, at, T_NEW_X + r, x_peer))
        new_core.append(send_new(1 - s, at, T_NEW_CORE + r, core_peer))
    for r in (2, 3, 0, 1):
        at = chunk(c, 1 - h, r)
        grad_x[r].wait()
        update(at)
        if r >= 2:
            new_y.append(send_new(s, at, T_NEW_Y + 2 + r, y_peer))
        grad_core.append(send_grad(at, T_GRAD_CORE + 4 + r, core_peer))
    for r in range(2, 4):
        new_y[r].wait()
        new_core.append(send_new(1 - s, chunk(c, h, r), T_NEW_CORE + r, core_peer))
    for copy in grad_core:
        copy.wait()
    for r in range(LINE):
        update(chunk(1 - c, h, r))
        update(chunk(1 - c, 1 - h, r))
    m1_out = pltpu.make_async_copy(m1, m1o_hbm, local_sem.at[OUT_M1])
    m1_out.start()
    m2_out = pltpu.make_async_copy(m2, m2o_hbm, local_sem.at[OUT_M2])
    m2_out.start()
    for r in range(2):
        new_x[r].wait()
        new_core.append(send_new(1 - s, chunk(c, 1 - h, r), T_NEW_CORE + 4 + r, core_peer))
    for r in range(2, 4):
        new_y[2 + r].wait()
        new_core.append(send_new(1 - s, chunk(c, 1 - h, r), T_NEW_CORE + 4 + r, core_peer))
    for copy in new_core:
        copy.wait()
    nw_out = pltpu.make_async_copy(nw, nw_hbm, local_sem.at[OUT_W])
    nw_out.start()
    for copy in ig_out:
        copy.wait()
    m1_out.wait()
    m2_out.wait()
    nw_out.wait()


def hand_over(*refs):
    sources, targets, sem = refs[:4], refs[4:8], refs[8]
    copies = []
    for i, (source, target) in enumerate(zip(sources, targets)):
        step = source.shape[0] // PIECES
        for j in range(PIECES):
            rows = pl.ds(j * step, step)
            copy = pltpu.make_async_copy(source.at[rows], target.at[rows], sem.at[i * PIECES + j])
            copy.start()
            copies.append(copy)
    for copy in copies:
        copy.wait()


def on_device(
    clips,
    code_grad,
    conv_weight,
    norm_gain,
    proj_weight,
    code_bias,
    rotation,
    first_moment,
    second_moment,
):
    count, frames, sites, width = clips.shape
    bits = code_grad.shape[3]
    dp_size = lax.axis_size("dp")
    devices = dp_size * lax.axis_size("shard")
    far_size = dp_size // DEPTH
    tokens = count * frames * sites
    rows, half = conv_weight.shape[0], first_moment.shape[0]
    per_core, per_x, own = half // 2, half // 4, half // DEPTH
    sizes = (
        count,
        frames,
        sites,
        width,
        bits,
        dp_size,
        far_size,
        tokens * devices,
        count * devices,
    )
    vmem = pltpu.VMEM
    scratch = [
        vmem((tokens, width), BF16),
        vmem((width, tokens), BF16),
        vmem((rows, width), BF16),
        vmem((rows, width), BF16),
        vmem((frames, bits, count, sites), BF16),
        vmem((tokens, width), F32),
        vmem((tokens, 1), F32),
        vmem((BITS_PAD, tokens), F32),
        vmem((BITS_PAD, tokens), F32),
        vmem((BITS_PAD, tokens), F32),
        vmem((128, tokens), F32),
        vmem((128, width), BF16),
        vmem((tokens, width), BF16),
        vmem((tokens, width), BF16),
        vmem((half, width), F32),
        vmem((half, width), F32),
        vmem((rows, width), F32),
        vmem((2, per_core, width), F32),
        vmem((2, per_x, width), F32),
        vmem((2, per_x, width), BF16),
        vmem((2, per_x, width), BF16),
        vmem((per_x, width), BF16),
        vmem((per_x, width), BF16),
        vmem((per_x, width), BF16),
        vmem((LINE, own, width), BF16),
        vmem((far_size, own, width), F32),
        vmem((half, width), BF16),
        vmem((rows, width), BF16),
        vmem((PLANE, BITS_PAD, 128), F32),
        vmem((LINE, BITS_PAD, 128), F32),
        vmem((far_size, BITS_PAD, 128), F32),
        pltpu.SemaphoreType.DMA((IN_X + 2 * count * frames,)),
        pltpu.SemaphoreType.DMA((T_FAR + 2 * far_size,)),
        pltpu.SemaphoreType.DMA((T_FAR + 2 * far_size,)),
    ]
    whole = pl.BlockSpec(memory_space=pltpu.VMEM)
    outside = pl.BlockSpec(memory_space=pl.ANY)
    *large, loss = pl.pallas_call(
        functools.partial(kernel, sizes),
        out_shape=(
            jax.ShapeDtypeStruct((rows, width), BF16),
            jax.ShapeDtypeStruct((half, width), F32),
            jax.ShapeDtypeStruct((half, width), F32),
            jax.ShapeDtypeStruct((tokens, width), BF16),
            jax.ShapeDtypeStruct((1, 1), F32),
        ),
        in_specs=[outside, outside, outside, whole, whole, whole, whole, outside, outside],
        out_specs=(outside, outside, outside, outside, whole),
        scratch_shapes=scratch,
        compiler_params=pltpu.CompilerParams(
            collective_id=0, has_side_effects=True, vmem_limit_bytes=VMEM_BYTES
        ),
    )(
        clips.reshape(tokens, width),
        code_grad.transpose(1, 3, 0, 2),
        conv_weight,
        norm_gain.reshape(1, width),
        proj_weight.T,
        code_bias.reshape(1, bits),
        rotation,
        first_moment,
        second_moment,
    )
    new_weight, first_out, second_out, input_grad = pl.pallas_call(
        hand_over,
        out_shape=tuple(jax.ShapeDtypeStruct(a.shape, a.dtype) for a in large),
        in_specs=[outside] * 4,
        out_specs=(outside,) * 4,
        scratch_shapes=[pltpu.SemaphoreType.DMA((4 * PIECES,))],
        compiler_params=pltpu.CompilerParams(vmem_limit_bytes=VMEM_BYTES),
    )(*large)
    return (
        new_weight,
        first_out,
        second_out,
        input_grad.reshape(clips.shape),
        loss.reshape(()),
    )


def solution(mesh):
    return jax.shard_map(
        on_device,
        mesh=mesh,
        in_specs=(
            P(("dp", "shard"), None, None, None),
            P(("dp", "shard"), None, None, None),
            P(),
            P(),
            P(),
            P(),
            P(),
            P("shard", None),
            P("shard", None),
        ),
        out_specs=(
            P(),
            P("shard", None),
            P("shard", None),
            P(("dp", "shard"), None, None, None),
            P(),
        ),
        check_vma=False,
    )
```

```python
import functools

import jax
import jax.numpy as jnp
from jax import lax
from jax.experimental import pallas as pl
from jax.experimental.pallas import tpu as pltpu
from jax.sharding import PartitionSpec as P

MESH = pl.DeviceIdType.MESH
F32 = jnp.float32
BF16 = jnp.bfloat16
HIGHEST = lax.Precision.HIGHEST
BITS_PAD = 32
PLANE = 8
LINE = 4
DEPTH = 16
PIECES = 4
VMEM_BYTES = 60 * 1024 * 1024

IN_W, IN_CG, IN_M1, IN_M2, OUT_W, OUT_M1, OUT_M2, IN_X = range(8)
(
    T_PLANE,
    T_LINE,
    T_CORE,
    T_FIRST,
    T_SECOND,
    T_ROWS,
    T_GATHER,
    T_GRAD_X,
    T_GRAD_CORE,
    T_NEW_Y,
    T_NEW_X,
    T_NEW_CORE,
    T_FAR,
) = (0, 8, 12, 14, 16, 17, 21, 25, 29, 37, 45, 47, 55)

NN = (((1,), (0,)), ((), ()))
NT = (((1,), (1,)), ((), ()))


def dot(a, b, dims=NN, precision=None):
    return lax.dot_general(a, b, dims, precision=precision, preferred_element_type=F32)


def flip(bit, change):
    return bit + (1 - 2 * bit) if change else bit


def kernel(
    sizes,
    clips_hbm,
    cg_hbm,
    weight_hbm,
    gain_ref,
    proj_ref,
    bias_ref,
    rot_ref,
    m1_hbm,
    m2_hbm,
    nw_hbm,
    m1o_hbm,
    m2o_hbm,
    ig_hbm,
    loss_ref,
    xs,
    xt,
    w,
    wt,
    cg,
    unit,
    inv,
    rott,
    cgt,
    dl,
    pp,
    dc,
    ig,
    m1,
    m2,
    g,
    r1,
    keep,
    s2,
    r2,
    s3,
    r3,
    s4,
    r4,
    far,
    gr,
    nw,
    stat,
    stat2,
    stat3,
    local_sem,
    send_sem,
    recv_sem,
):
    clips, frames, sites, width, bits, dp_size, far_size, tokens_all, clips_all = sizes
    clip_rows = frames * sites
    block = clips * sites
    half = m1.shape[0]
    per_core, per_x = half // 2, half // 4
    own = half // DEPTH
    dp = lax.axis_index("dp")
    s = lax.axis_index("shard")
    c = dp % 2
    h = (dp // 2) % 2
    z = (dp // 4) % 4
    z0, z1 = z % 2, z // 2
    f = dp // DEPTH

    def plane_peer(r):
        return (dp - c - 2 * h + flip(c, r & 1) + 2 * flip(h, r & 2), flip(s, r & 4))

    def line_at(r):
        return flip(z0, r & 1) + 2 * flip(z1, r & 2)

    def line_peer(r):
        return (dp + 4 * (line_at(r) - z), s)

    def far_at(r):
        return (f + r) % far_size

    def far_peer(r):
        return (dp + DEPTH * (far_at(r) - f), s)

    def send(src, dst, index, peer):
        copy = pltpu.make_async_remote_copy(
            src_ref=src,
            dst_ref=dst,
            send_sem=send_sem.at[index],
            recv_sem=recv_sem.at[index],
            device_id=peer,
            device_id_type=MESH,
        )
        copy.start()
        return copy

    w_in = pltpu.make_async_copy(weight_hbm, w, local_sem.at[IN_W])
    w_in.start()
    x_in = []
    for frame in range(frames):
        for clip in range(clips):
            copy = pltpu.make_async_copy(
                clips_hbm.at[pl.ds(clip * clip_rows + frame * sites, sites)],
                xs.at[pl.ds(frame * block + clip * sites, sites)],
                local_sem.at[IN_X + frame * clips + clip],
            )
            copy.start()
            x_in.append(copy)
    cg_in = pltpu.make_async_copy(cg_hbm, cg, local_sem.at[IN_CG])
    cg_in.start()
    m1_in = pltpu.make_async_copy(m1_hbm, m1, local_sem.at[IN_M1])
    m1_in.start()
    m2_in = pltpu.make_async_copy(m2_hbm, m2, local_sem.at[IN_M2])
    m2_in.start()

    barrier = pltpu.get_barrier_semaphore()
    peers = [plane_peer(r) for r in range(1, PLANE)]
    peers += [line_peer(r) for r in range(1, LINE)]
    for r in range(1, far_size):
        peers.append(far_peer(r))
    for peer in peers:
        pl.semaphore_signal(barrier, inc=1, device_id=peer, device_id_type=MESH)

    eye_mask = lax.broadcasted_iota(jnp.int32, (BITS_PAD, bits), 0) == lax.broadcasted_iota(
        jnp.int32, (BITS_PAD, bits), 1
    )
    eye = jnp.where(eye_mask, 1.0, 0.0).astype(F32)
    eye16 = eye.astype(BF16)
    rot_rows = dot(eye, rot_ref[...], NN, HIGHEST)
    rot_t = dot(eye, rot_rows, NT, HIGHEST)
    proj_t = dot(rot_t, dot(eye16, proj_ref[...]), NN, HIGHEST)
    proj_high = proj_t.astype(BF16)
    proj_low = (proj_t - proj_high.astype(F32)).astype(BF16)
    pp[...] = jnp.zeros_like(pp)
    pp[0:BITS_PAD, :] = proj_high
    pp[BITS_PAD : 2 * BITS_PAD, :] = proj_low
    pp[2 * BITS_PAD : 3 * BITS_PAD, :] = proj_high
    dl[...] = jnp.zeros_like(dl)
    bias = jnp.sum(jnp.where(eye_mask, bias_ref[...], 0.0), axis=1, keepdims=True)
    bias = dot(rot_t, jnp.broadcast_to(bias, (BITS_PAD, 128)), NN, HIGHEST)[:, 0:1]
    gain = gain_ref[...]

    w_in.wait()

    for frame in range(frames):
        here = slice(frame * block, (frame + 1) * block)
        for copy in x_in[frame * clips : (frame + 1) * clips]:
            copy.wait()
        taps = min(frame, 2) + 1
        parts = [xs[(frame - k) * block : (frame - k + 1) * block, :] for k in range(taps)]
        lhs = parts[0] if taps == 1 else jnp.concatenate(parts, axis=1)
        hidden = parts[0].astype(F32) + dot(lhs, w[0 : taps * width, :])
        scale = lax.rsqrt(jnp.mean(hidden * hidden, axis=1, keepdims=True) + 1e-06)
        u = hidden * scale
        unit[here, :] = u
        inv[here, :] = scale
        normed = (u * gain).astype(BF16)
        both = dot(pp[0 : 2 * BITS_PAD, :], normed, NT)
        rott[:, here] = both[0:BITS_PAD, :] + both[BITS_PAD:, :] + bias
        xt[:, here] = xs[here, :].T

    cg_in.wait()
    cgt[...] = jnp.zeros_like(cgt)
    for frame in range(frames):
        value = cg[frame].astype(F32)
        for clip in range(clips):
            start = frame * block + clip * sites
            cgt[0:bits, start : start + sites] = value[:, clip, :]
    rotated = rott[...]
    cotangent = cgt[...]
    codes = jnp.tanh(rotated)
    probs = (1.0 + codes) / 2.0
    logit = 2.0 * rotated
    softplus = jnp.maximum(logit, 0.0) + jnp.log(1.0 + jnp.exp(-jnp.abs(logit)))
    entropy = softplus - logit * probs
    token_loss = cotangent * codes + 0.25 * (rotated - codes) ** 2 + 0.1 * entropy
    real = lax.broadcasted_iota(jnp.int32, (BITS_PAD, 1), 0) < bits
    loss_part = jnp.sum(
        jnp.where(real, jnp.sum(token_loss, axis=1, keepdims=True), 0.0), axis=0, keepdims=True
    )
    bit_part = jnp.sum(probs, axis=1, keepdims=True)
    column = jnp.where(real, bit_part, loss_part)
    stat[0] = jnp.broadcast_to(column, stat.shape[1:])

    pl.semaphore_wait(barrier, len(peers))
    sent = [send(stat.at[0], stat.at[r], T_PLANE + r, plane_peer(r)) for r in range(1, PLANE)]

    slope = 1.0 - codes * codes
    base = (
        cotangent * slope
        + 0.5 * (rotated - codes) * (1.0 - slope)
        - 0.2 * logit * probs * (1.0 - probs)
    )
    rott[...] = base / clips_all
    cgt[...] = 0.05 * slope / clips_all
    for k in range(3):
        wt[k * width : (k + 1) * width, :] = w[k * width : (k + 1) * width, :].T
    for copy in sent:
        copy.wait()
    total = stat[0]
    for r in range(1, PLANE):
        total = total + stat[r]
    stat2[0] = total
    sent = [send(stat2.at[0], stat2.at[r], T_LINE + r, line_peer(r)) for r in range(1, LINE)]

    for copy in sent:
        copy.wait()
    total = stat2[0]
    for r in range(1, LINE):
        total = total + stat2[r]
    if far_size > 1:
        stat3[f] = total
        sent = [
            send(stat3.at[f], stat3.at[f], T_FAR + r, far_peer(r)) for r in range(1, far_size)
        ]
        for copy in sent:
            copy.wait()
        total = stat3[0]
        for r in range(1, far_size):
            total = total + stat3[r]
    total = total[:, 0:1]
    bit_mean = jnp.where(real, total / tokens_all, 0.5)
    code_entropy = -bit_mean * jnp.log(bit_mean) - (1.0 - bit_mean) * jnp.log(1.0 - bit_mean)
    code_entropy = jnp.sum(jnp.where(real, code_entropy, 0.0), axis=0, keepdims=True)
    loss_ref[...] = total[bits : bits + 1, :] / tokens_all - 0.1 * code_entropy
    lean = jnp.log((1.0 - bit_mean) / bit_mean)

    d_rot = rott[...] - cgt[...] * lean
    high = d_rot.astype(BF16).astype(F32)
    dl[0:BITS_PAD, :] = high
    dl[BITS_PAD : 2 * BITS_PAD, :] = high
    dl[2 * BITS_PAD : 3 * BITS_PAD, :] = d_rot - high

    for frame in range(frames):
        here = slice(frame * block, (frame + 1) * block)
        a = dot(dl[:, here].T.astype(BF16), pp[...]) * gain
        u = unit[here, :]
        d_hidden = inv[here, :] * (a - u * jnp.mean(a * u, axis=1, keepdims=True))
        dc[here, :] = d_hidden.astype(BF16)

    core_peer = plane_peer(1)
    core_sent = []
    for k in range(3):
        g[k * width : (k + 1) * width, :] = dot(xt[:, 0 : (frames - k) * block], dc[k * block :, :])
        for j in range(2):
            if (k + 1) * width >= (j + 1) * half > k * width:
                rows = pl.ds(pl.multiple_of(j * half + (1 - c) * per_core, 8), per_core)
                core_sent.append(send(g.at[rows], r1.at[j], T_CORE + j, core_peer))

    ig_out = []

    def input_grad(frame):
        here = slice(frame * block, (frame + 1) * block)
        taps = min(frames - 1 - frame, 2) + 1
        parts = [dc[(frame + k) * block : (frame + k + 1) * block, :] for k in range(taps)]
        lhs = parts[0] if taps == 1 else jnp.concatenate(parts, axis=1)
        ig[here, :] = (parts[0].astype(F32) + dot(lhs, wt[0 : taps * width, :])).astype(BF16)
        for clip in range(clips):
            copy = pltpu.make_async_copy(
                ig.at[pl.ds(frame * block + clip * sites, sites)],
                ig_hbm.at[pl.ds(clip * clip_rows + frame * sites, sites)],
                local_sem.at[IN_X + (frames + frame) * clips + clip],
            )
            copy.start()
            ig_out.append(copy)

    input_grad(0)
    for copy in core_sent:
        copy.wait()

    first_peer = (dp + (1 - c) * 2 * (1 - 2 * h), s + c * (1 - 2 * s))
    second_peer = (dp + c * 2 * (1 - 2 * h), s + (1 - c) * (1 - 2 * s))

    def summed(side, x):
        rows = pl.ds(pl.multiple_of(side * half + c * per_core + x * per_x, 8), per_x)
        return g[rows, :] + r1[side, pl.ds(pl.multiple_of(x * per_x, 8), per_x), :]

    kept = (1 - c) * s + c * h
    first_sent = []
    for i, j in enumerate((1 - kept, kept)):
        s2[j] = summed((1 - c) * j + c * (1 - s), (1 - c) * (1 - h) + c * j).astype(BF16)
        first_sent.append(send(s2.at[j], r2.at[j], T_FIRST + i, first_peer))
    for j in range(2):
        keep[j] = summed((1 - c) * j + c * s, (1 - c) * h + c * j)
    input_grad(1)
    first_sent[0].wait()
    s3[...] = (keep[1 - kept] + r2[1 - kept].astype(F32)).astype(BF16)
    second_sent = send(s3, r3, T_SECOND, second_peer)
    input_grad(2)
    m1_in.wait()
    m2_in.wait()
    first_sent[1].wait()
    keep[kept] = keep[kept] + r2[kept].astype(F32)
    second_sent.wait()
    mine = keep[kept] + r3[...].astype(F32)
    s4[...] = mine.astype(BF16)
    keep[kept] = mine
    rows_sent = []
    for r in range(1, LINE):
        rows = pl.ds(pl.multiple_of(line_at(r) * own, 16), own)
        rows_sent.append(send(s4.at[rows], r4.at[r], T_ROWS + r, line_peer(r)))
    for frame in range(3, frames):
        input_grad(frame)
    for copy in rows_sent:
        copy.wait()
    grad = keep[kept, pl.ds(pl.multiple_of(z * own, 8), own), :]
    for r in range(1, LINE):
        grad = grad + r4[r].astype(F32)
    if far_size > 1:
        far[f] = grad
        sent = [
            send(far.at[f], far.at[f], T_FAR + far_size + r, far_peer(r))
            for r in range(1, far_size)
        ]
        for copy in sent:
            copy.wait()
        grad = far[0]
        for r in range(1, far_size):
            grad = grad + far[r]

    def chunk(core, x, r):
        return core * per_core + x * per_x + line_at(r) * own

    def update(at):
        rows = pl.ds(pl.multiple_of(at, 16), own)
        here = pl.ds(pl.multiple_of(s * half + at, 16), own)
        value = gr[rows, :].astype(F32)
        first = 0.9 * m1[rows, :] + 0.1 * value
        second = 0.99 * m2[rows, :] + 0.01 * value * value
        m1[rows, :] = first
        m2[rows, :] = second
        stepped = w[here, :].astype(F32) - 0.001 * first / (jnp.sqrt(second) + 1e-08)
        nw[here, :] = stepped.astype(BF16)

    def send_grad(at, index, peer):
        rows = gr.at[pl.ds(pl.multiple_of(at, 16), own)]
        return send(rows, rows, index, peer)

    def send_new(side, at, index, peer):
        rows = nw.at[pl.ds(pl.multiple_of(side * half + at, 16), own)]
        return send(rows, rows, index, peer)

    x_peer, y_peer = plane_peer(2), plane_peer(4)
    own_at = chunk(c, h, 0)
    gr[pl.ds(pl.multiple_of(own_at, 16), own), :] = grad.astype(BF16)
    gather = [send_grad(own_at, T_GATHER + r, line_peer(r)) for r in range(1, LINE)]
    grad_x, grad_core, new_y, new_x, new_core = [], [], [], [], []
    for r in range(LINE):
        at = chunk(c, h, r)
        if r > 0:
            gather[r - 1].wait()
        grad_x.append(send_grad(at, T_GRAD_X + r, x_peer))
        update(at)
        new_y.append(send_new(s, at, T_NEW_Y + r, y_peer))
        grad_core.append(send_grad(at, T_GRAD_CORE + r, core_peer))
    for r in range(2):
        at = chunk(c, h, r)
        new_y[r].wait()
        new_x.append(send_new(1 - s, at, T_NEW_X + r, x_peer))
        new_core.append(send_new(1 - s, at, T_NEW_CORE + r, core_peer))
    for r in (2, 3, 0, 1):
        at = chunk(c, 1 - h, r)
        grad_x[r].wait()
        update(at)
        if r >= 2:
            new_y.append(send_new(s, at, T_NEW_Y + 2 + r, y_peer))
        grad_core.append(send_grad(at, T_GRAD_CORE + 4 + r, core_peer))
    for r in range(2, 4):
        new_y[r].wait()
        new_core.append(send_new(1 - s, chunk(c, h, r), T_NEW_CORE + r, core_peer))
    for copy in grad_core:
        copy.wait()
    for r in range(LINE):
        update(chunk(1 - c, h, r))
        update(chunk(1 - c, 1 - h, r))
    m1_out = pltpu.make_async_copy(m1, m1o_hbm, local_sem.at[OUT_M1])
    m1_out.start()
    m2_out = pltpu.make_async_copy(m2, m2o_hbm, local_sem.at[OUT_M2])
    m2_out.start()
    for r in range(2):
        new_x[r].wait()
        new_core.append(send_new(1 - s, chunk(c, 1 - h, r), T_NEW_CORE + 4 + r, core_peer))
    for r in range(2, 4):
        new_y[2 + r].wait()
        new_core.append(send_new(1 - s, chunk(c, 1 - h, r), T_NEW_CORE + 4 + r, core_peer))
    for copy in new_core:
        copy.wait()
    nw_out = pltpu.make_async_copy(nw, nw_hbm, local_sem.at[OUT_W])
    nw_out.start()
    for copy in ig_out:
        copy.wait()
    m1_out.wait()
    m2_out.wait()
    nw_out.wait()


def hand_over(*refs):
    sources, targets, stages, in_sem, out_sem = refs[:4], refs[4:8], refs[8:12], refs[12], refs[13]
    loads, stores = [], []
    for i, (source, stage) in enumerate(zip(sources, stages)):
        step = source.shape[0] // PIECES
        for j in range(PIECES):
            rows = pl.ds(j * step, step)
            index = i * PIECES + j
            load = pltpu.make_async_copy(source.at[rows], stage.at[rows], in_sem.at[index])
            load.start()
            loads.append(load)
            store = pltpu.make_async_copy(stage.at[rows], targets[i].at[rows], out_sem.at[index])
            stores.append(store)
    for load, store in zip(loads, stores):
        load.wait()
        store.start()
    for store in stores:
        store.wait()


def on_device(
    clips,
    code_grad,
    conv_weight,
    norm_gain,
    proj_weight,
    code_bias,
    rotation,
    first_moment,
    second_moment,
):
    count, frames, sites, width = clips.shape
    bits = code_grad.shape[3]
    dp_size = lax.axis_size("dp")
    devices = dp_size * lax.axis_size("shard")
    far_size = dp_size // DEPTH
    tokens = count * frames * sites
    rows, half = conv_weight.shape[0], first_moment.shape[0]
    per_core, per_x, own = half // 2, half // 4, half // DEPTH
    sizes = (
        count,
        frames,
        sites,
        width,
        bits,
        dp_size,
        far_size,
        tokens * devices,
        count * devices,
    )
    vmem = pltpu.VMEM
    scratch = [
        vmem((tokens, width), BF16),
        vmem((width, tokens), BF16),
        vmem((rows, width), BF16),
        vmem((rows, width), BF16),
        vmem((frames, bits, count, sites), BF16),
        vmem((tokens, width), F32),
        vmem((tokens, 1), F32),
        vmem((BITS_PAD, tokens), F32),
        vmem((BITS_PAD, tokens), F32),
        vmem((128, tokens), F32),
        vmem((128, width), BF16),
        vmem((tokens, width), BF16),
        vmem((tokens, width), BF16),
        vmem((half, width), F32),
        vmem((half, width), F32),
        vmem((rows, width), F32),
        vmem((2, per_core, width), F32),
        vmem((2, per_x, width), F32),
        vmem((2, per_x, width), BF16),
        vmem((2, per_x, width), BF16),
        vmem((per_x, width), BF16),
        vmem((per_x, width), BF16),
        vmem((per_x, width), BF16),
        vmem((LINE, own, width), BF16),
        vmem((far_size, own, width), F32),
        vmem((half, width), BF16),
        vmem((rows, width), BF16),
        vmem((PLANE, BITS_PAD, 128), F32),
        vmem((LINE, BITS_PAD, 128), F32),
        vmem((far_size, BITS_PAD, 128), F32),
        pltpu.SemaphoreType.DMA((IN_X + 2 * count * frames,)),
        pltpu.SemaphoreType.DMA((T_FAR + 2 * far_size,)),
        pltpu.SemaphoreType.DMA((T_FAR + 2 * far_size,)),
    ]
    whole = pl.BlockSpec(memory_space=pltpu.VMEM)
    outside = pl.BlockSpec(memory_space=pl.ANY)
    *large, loss = pl.pallas_call(
        functools.partial(kernel, sizes),
        out_shape=(
            jax.ShapeDtypeStruct((rows, width), BF16),
            jax.ShapeDtypeStruct((half, width), F32),
            jax.ShapeDtypeStruct((half, width), F32),
            jax.ShapeDtypeStruct((tokens, width), BF16),
            jax.ShapeDtypeStruct((1, 1), F32),
        ),
        in_specs=[outside, outside, outside, whole, whole, whole, whole, outside, outside],
        out_specs=(outside, outside, outside, outside, whole),
        scratch_shapes=scratch,
        compiler_params=pltpu.CompilerParams(
            collective_id=0, has_side_effects=True, vmem_limit_bytes=VMEM_BYTES
        ),
    )(
        clips.reshape(tokens, width),
        code_grad.transpose(1, 3, 0, 2),
        conv_weight,
        norm_gain.reshape(1, width),
        proj_weight.T,
        code_bias.reshape(1, bits),
        rotation,
        first_moment,
        second_moment,
    )
    new_weight, first_out, second_out, input_grad = pl.pallas_call(
        hand_over,
        out_shape=tuple(jax.ShapeDtypeStruct(a.shape, a.dtype) for a in large),
        in_specs=[outside] * 4,
        out_specs=(outside,) * 4,
        scratch_shapes=[vmem(a.shape, a.dtype) for a in large]
        + [pltpu.SemaphoreType.DMA((4 * PIECES,))] * 2,
        compiler_params=pltpu.CompilerParams(vmem_limit_bytes=VMEM_BYTES),
    )(*large)
    return (
        new_weight,
        first_out,
        second_out,
        input_grad.reshape(clips.shape),
        loss.reshape(()),
    )


def solution(mesh):
    return jax.shard_map(
        on_device,
        mesh=mesh,
        in_specs=(
            P(("dp", "shard"), None, None, None),
            P(("dp", "shard"), None, None, None),
            P(),
            P(),
            P(),
            P(),
            P(),
            P("shard", None),
            P("shard", None),
        ),
        out_specs=(
            P(),
            P("shard", None),
            P("shard", None),
            P(("dp", "shard"), None, None, None),
            P(),
        ),
        check_vma=False,
    )
```

```python
import functools

import jax
import jax.numpy as jnp
from jax import lax
from jax.experimental import pallas as pl
from jax.experimental.pallas import tpu as pltpu
from jax.sharding import PartitionSpec as P

MESH = pl.DeviceIdType.MESH
F32 = jnp.float32
BF16 = jnp.bfloat16
HIGHEST = lax.Precision.HIGHEST
BITS_PAD = 32
PLANE = 8
LINE = 4
DEPTH = 16
PIECES = 4
VMEM_BYTES = 60 * 1024 * 1024

IN_W, IN_CG, IN_M1, IN_M2, OUT_W, OUT_M1, OUT_M2, IN_X = range(8)
(
    T_PLANE,
    T_LINE,
    T_CORE,
    T_FIRST,
    T_SECOND,
    T_ROWS,
    T_GATHER,
    T_GRAD_X,
    T_GRAD_CORE,
    T_NEW_Y,
    T_NEW_X,
    T_NEW_CORE,
    T_FAR,
) = (0, 8, 12, 14, 16, 17, 21, 25, 29, 37, 45, 47, 55)

NN = (((1,), (0,)), ((), ()))
NT = (((1,), (1,)), ((), ()))


def dot(a, b, dims=NN, precision=None):
    return lax.dot_general(a, b, dims, precision=precision, preferred_element_type=F32)


def flip(bit, change):
    return bit + (1 - 2 * bit) if change else bit


def kernel(
    sizes,
    clips_hbm,
    cg_hbm,
    weight_hbm,
    gain_ref,
    proj_ref,
    bias_ref,
    rot_ref,
    m1_hbm,
    m2_hbm,
    nw_hbm,
    m1o_hbm,
    m2o_hbm,
    ig_hbm,
    loss_ref,
    xs,
    xt,
    w,
    wt,
    cg,
    unit,
    inv,
    rott,
    cgt,
    dl,
    pp,
    dc,
    ig,
    m1,
    m2,
    g,
    gs,
    r1,
    keep,
    s2,
    r2,
    s3,
    r3,
    s4,
    r4,
    far,
    gr,
    nw,
    stat,
    stat2,
    stat3,
    local_sem,
    send_sem,
    recv_sem,
):
    clips, frames, sites, width, bits, dp_size, far_size, tokens_all, clips_all = sizes
    clip_rows = frames * sites
    block = clips * sites
    half = m1.shape[0]
    per_x = half // 2
    own = per_x // LINE
    cols = width // 2
    dp = lax.axis_index("dp")
    s = lax.axis_index("shard")
    c = dp % 2
    h = (dp // 2) % 2
    z = (dp // 4) % 4
    z0, z1 = z % 2, z // 2
    f = dp // DEPTH

    def plane_peer(r):
        return (dp - c - 2 * h + flip(c, r & 1) + 2 * flip(h, r & 2), flip(s, r & 4))

    def line_at(r):
        return flip(z0, r & 1) + 2 * flip(z1, r & 2)

    def line_peer(r):
        return (dp + 4 * (line_at(r) - z), s)

    def far_at(r):
        return (f + r) % far_size

    def far_peer(r):
        return (dp + DEPTH * (far_at(r) - f), s)

    def send(src, dst, index, peer):
        copy = pltpu.make_async_remote_copy(
            src_ref=src,
            dst_ref=dst,
            send_sem=send_sem.at[index],
            recv_sem=recv_sem.at[index],
            device_id=peer,
            device_id_type=MESH,
        )
        copy.start()
        return copy

    w_in = pltpu.make_async_copy(weight_hbm, w, local_sem.at[IN_W])
    w_in.start()
    x_in = []
    for frame in range(frames):
        for clip in range(clips):
            copy = pltpu.make_async_copy(
                clips_hbm.at[pl.ds(clip * clip_rows + frame * sites, sites)],
                xs.at[pl.ds(frame * block + clip * sites, sites)],
                local_sem.at[IN_X + frame * clips + clip],
            )
            copy.start()
            x_in.append(copy)
    cg_in = pltpu.make_async_copy(cg_hbm, cg, local_sem.at[IN_CG])
    cg_in.start()
    m1_in = pltpu.make_async_copy(m1_hbm, m1, local_sem.at[IN_M1])
    m1_in.start()
    m2_in = pltpu.make_async_copy(m2_hbm, m2, local_sem.at[IN_M2])
    m2_in.start()

    barrier = pltpu.get_barrier_semaphore()
    peers = [plane_peer(r) for r in range(1, PLANE)]
    peers += [line_peer(r) for r in range(1, LINE)]
    for r in range(1, far_size):
        peers.append(far_peer(r))
    for peer in peers:
        pl.semaphore_signal(barrier, inc=1, device_id=peer, device_id_type=MESH)

    eye_mask = lax.broadcasted_iota(jnp.int32, (BITS_PAD, bits), 0) == lax.broadcasted_iota(
        jnp.int32, (BITS_PAD, bits), 1
    )
    eye = jnp.where(eye_mask, 1.0, 0.0).astype(F32)
    eye16 = eye.astype(BF16)
    rot_rows = dot(eye, rot_ref[...], NN, HIGHEST)
    rot_t = dot(eye, rot_rows, NT, HIGHEST)
    proj_t = dot(rot_t, dot(eye16, proj_ref[...]), NN, HIGHEST)
    proj_high = proj_t.astype(BF16)
    proj_low = (proj_t - proj_high.astype(F32)).astype(BF16)
    pp[...] = jnp.zeros_like(pp)
    pp[0:BITS_PAD, :] = proj_high
    pp[BITS_PAD : 2 * BITS_PAD, :] = proj_low
    pp[2 * BITS_PAD : 3 * BITS_PAD, :] = proj_high
    dl[...] = jnp.zeros_like(dl)
    bias = jnp.sum(jnp.where(eye_mask, bias_ref[...], 0.0), axis=1, keepdims=True)
    bias = dot(rot_t, jnp.broadcast_to(bias, (BITS_PAD, 128)), NN, HIGHEST)[:, 0:1]
    gain = gain_ref[...]

    w_in.wait()

    for frame in range(frames):
        here = slice(frame * block, (frame + 1) * block)
        for copy in x_in[frame * clips : (frame + 1) * clips]:
            copy.wait()
        taps = min(frame, 2) + 1
        parts = [xs[(frame - k) * block : (frame - k + 1) * block, :] for k in range(taps)]
        lhs = parts[0] if taps == 1 else jnp.concatenate(parts, axis=1)
        hidden = parts[0].astype(F32) + dot(lhs, w[0 : taps * width, :])
        scale = lax.rsqrt(jnp.mean(hidden * hidden, axis=1, keepdims=True) + 1e-06)
        u = hidden * scale
        unit[here, :] = u
        inv[here, :] = scale
        normed = (u * gain).astype(BF16)
        both = dot(pp[0 : 2 * BITS_PAD, :], normed, NT)
        rott[:, here] = both[0:BITS_PAD, :] + both[BITS_PAD:, :] + bias
        xt[:, here] = xs[here, :].T

    cg_in.wait()
    cgt[...] = jnp.zeros_like(cgt)
    for frame in range(frames):
        value = cg[frame].astype(F32)
        for clip in range(clips):
            start = frame * block + clip * sites
            cgt[0:bits, start : start + sites] = value[:, clip, :]
    rotated = rott[...]
    cotangent = cgt[...]
    codes = jnp.tanh(rotated)
    probs = (1.0 + codes) / 2.0
    logit = 2.0 * rotated
    softplus = jnp.maximum(logit, 0.0) + jnp.log(1.0 + jnp.exp(-jnp.abs(logit)))
    entropy = softplus - logit * probs
    token_loss = cotangent * codes + 0.25 * (rotated - codes) ** 2 + 0.1 * entropy
    real = lax.broadcasted_iota(jnp.int32, (BITS_PAD, 1), 0) < bits
    loss_part = jnp.sum(
        jnp.where(real, jnp.sum(token_loss, axis=1, keepdims=True), 0.0), axis=0, keepdims=True
    )
    bit_part = jnp.sum(probs, axis=1, keepdims=True)
    column = jnp.where(real, bit_part, loss_part)
    stat[0] = jnp.broadcast_to(column, stat.shape[1:])

    pl.semaphore_wait(barrier, len(peers))
    sent = [send(stat.at[0], stat.at[r], T_PLANE + r, plane_peer(r)) for r in range(1, PLANE)]

    slope = 1.0 - codes * codes
    base = (
        cotangent * slope
        + 0.5 * (rotated - codes) * (1.0 - slope)
        - 0.2 * logit * probs * (1.0 - probs)
    )
    rott[...] = base / clips_all
    cgt[...] = 0.05 * slope / clips_all
    for k in range(3):
        wt[k * width : (k + 1) * width, :] = w[k * width : (k + 1) * width, :].T
    for copy in sent:
        copy.wait()
    total = stat[0]
    for r in range(1, PLANE):
        total = total + stat[r]
    stat2[0] = total
    sent = [send(stat2.at[0], stat2.at[r], T_LINE + r, line_peer(r)) for r in range(1, LINE)]

    for copy in sent:
        copy.wait()
    total = stat2[0]
    for r in range(1, LINE):
        total = total + stat2[r]
    if far_size > 1:
        stat3[f] = total
        sent = [
            send(stat3.at[f], stat3.at[f], T_FAR + r, far_peer(r)) for r in range(1, far_size)
        ]
        for copy in sent:
            copy.wait()
        total = stat3[0]
        for r in range(1, far_size):
            total = total + stat3[r]
    total = total[:, 0:1]
    bit_mean = jnp.where(real, total / tokens_all, 0.5)
    code_entropy = -bit_mean * jnp.log(bit_mean) - (1.0 - bit_mean) * jnp.log(1.0 - bit_mean)
    code_entropy = jnp.sum(jnp.where(real, code_entropy, 0.0), axis=0, keepdims=True)
    loss_ref[...] = total[bits : bits + 1, :] / tokens_all - 0.1 * code_entropy
    lean = jnp.log((1.0 - bit_mean) / bit_mean)

    d_rot = rott[...] - cgt[...] * lean
    high = d_rot.astype(BF16).astype(F32)
    dl[0:BITS_PAD, :] = high
    dl[BITS_PAD : 2 * BITS_PAD, :] = high
    dl[2 * BITS_PAD : 3 * BITS_PAD, :] = d_rot - high

    for frame in range(frames):
        here = slice(frame * block, (frame + 1) * block)
        a = dot(dl[:, here].T.astype(BF16), pp[...]) * gain
        u = unit[here, :]
        d_hidden = inv[here, :] * (a - u * jnp.mean(a * u, axis=1, keepdims=True))
        dc[here, :] = d_hidden.astype(BF16)

    core_peer = plane_peer(1)
    core_sent = []

    def columns(core):
        return pl.ds(pl.multiple_of(core * cols, cols), cols)

    def term(k, core):
        return dot(xt[:, 0 : (frames - k) * block], dc[k * block :, columns(core)])

    for k in range(3):
        gs[k * width : (k + 1) * width, :] = term(k, 1 - c).astype(BF16)
        for j in range(2):
            if (k + 1) * width >= (j + 1) * half > k * width:
                rows = slice(j * half, (j + 1) * half)
                core_sent.append(send(gs.at[rows], r1.at[rows], T_CORE + j, core_peer))
    for k in range(3):
        g[k * width : (k + 1) * width, :] = term(k, c)

    ig_out = []

    def input_grad(frame):
        here = slice(frame * block, (frame + 1) * block)
        taps = min(frames - 1 - frame, 2) + 1
        parts = [dc[(frame + k) * block : (frame + k + 1) * block, :] for k in range(taps)]
        lhs = parts[0] if taps == 1 else jnp.concatenate(parts, axis=1)
        ig[here, :] = (parts[0].astype(F32) + dot(lhs, wt[0 : taps * width, :])).astype(BF16)
        for clip in range(clips):
            copy = pltpu.make_async_copy(
                ig.at[pl.ds(frame * block + clip * sites, sites)],
                ig_hbm.at[pl.ds(clip * clip_rows + frame * sites, sites)],
                local_sem.at[IN_X + (frames + frame) * clips + clip],
            )
            copy.start()
            ig_out.append(copy)

    for copy in core_sent:
        copy.wait()

    first_peer = (dp + (1 - c) * 2 * (1 - 2 * h), s + c * (1 - 2 * s))
    second_peer = (dp + c * 2 * (1 - 2 * h), s + (1 - c) * (1 - 2 * s))

    def summed(side, x):
        rows = pl.ds(pl.multiple_of(side * half + x * per_x, 16), per_x)
        return g[rows, :] + r1[rows, :].astype(F32)

    kept = (1 - c) * s + c * h
    first_sent = []
    for i, j in enumerate((1 - kept, kept)):
        s2[j] = summed((1 - c) * j + c * (1 - s), (1 - c) * (1 - h) + c * j).astype(BF16)
        first_sent.append(send(s2.at[j], r2.at[j], T_FIRST + i, first_peer))
    for j in range(2):
        keep[j] = summed((1 - c) * j + c * s, (1 - c) * h + c * j)
    input_grad(0)
    input_grad(1)
    first_sent[0].wait()
    s3[...] = (keep[1 - kept] + r2[1 - kept].astype(F32)).astype(BF16)
    second_sent = send(s3, r3, T_SECOND, second_peer)
    input_grad(2)
    m1_in.wait()
    m2_in.wait()
    first_sent[1].wait()
    keep[kept] = keep[kept] + r2[kept].astype(F32)
    second_sent.wait()
    mine = keep[kept] + r3[...].astype(F32)
    s4[...] = mine.astype(BF16)
    keep[kept] = mine
    rows_sent = []
    for r in range(1, LINE):
        rows = pl.ds(pl.multiple_of(line_at(r) * own, 16), own)
        rows_sent.append(send(s4.at[rows], r4.at[r], T_ROWS + r, line_peer(r)))
    for frame in range(3, frames):
        input_grad(frame)
    for copy in rows_sent:
        copy.wait()
    grad = keep[kept, pl.ds(pl.multiple_of(z * own, 8), own), :]
    for r in range(1, LINE):
        grad = grad + r4[r].astype(F32)
    if far_size > 1:
        far[f] = grad
        sent = [
            send(far.at[f], far.at[f], T_FAR + far_size + r, far_peer(r))
            for r in range(1, far_size)
        ]
        for copy in sent:
            copy.wait()
        grad = far[0]
        for r in range(1, far_size):
            grad = grad + far[r]

    def chunk(x, r):
        return x * per_x + line_at(r) * own

    def update(core, at):
        rows = pl.ds(pl.multiple_of(at, 16), own)
        here = pl.ds(pl.multiple_of(s * half + at, 16), own)
        value = gr[core, rows, :].astype(F32)
        first = 0.9 * m1[rows, columns(core)] + 0.1 * value
        second = 0.99 * m2[rows, columns(core)] + 0.01 * value * value
        m1[rows, columns(core)] = first
        m2[rows, columns(core)] = second
        stepped = w[here, columns(core)].astype(F32) - 0.001 * first / (jnp.sqrt(second) + 1e-08)
        nw[core, here, :] = stepped.astype(BF16)

    def send_grad(at, index, peer):
        rows = gr.at[c, pl.ds(pl.multiple_of(at, 16), own)]
        return send(rows, rows, index, peer)

    def send_new(side, at, index, peer):
        rows = nw.at[c, pl.ds(pl.multiple_of(side * half + at, 16), own)]
        return send(rows, rows, index, peer)

    x_peer, y_peer = plane_peer(2), plane_peer(4)
    own_at = chunk(h, 0)
    gr[c, pl.ds(pl.multiple_of(own_at, 16), own), :] = grad.astype(BF16)
    gather = [send_grad(own_at, T_GATHER + r, line_peer(r)) for r in range(1, LINE)]
    grad_x, grad_core, new_y, new_x, new_core = [], [], [], [], []
    for r in range(LINE):
        at = chunk(h, r)
        if r > 0:
            gather[r - 1].wait()
        grad_x.append(send_grad(at, T_GRAD_X + r, x_peer))
        update(c, at)
        new_y.append(send_new(s, at, T_NEW_Y + r, y_peer))
        grad_core.append(send_grad(at, T_GRAD_CORE + r, core_peer))
    for r in range(2):
        at = chunk(h, r)
        new_y[r].wait()
        new_x.append(send_new(1 - s, at, T_NEW_X + r, x_peer))
        new_core.append(send_new(1 - s, at, T_NEW_CORE + r, core_peer))
    for r in (2, 3, 0, 1):
        at = chunk(1 - h, r)
        grad_x[r].wait()
        update(c, at)
        if r >= 2:
            new_y.append(send_new(s, at, T_NEW_Y + 2 + r, y_peer))
        grad_core.append(send_grad(at, T_GRAD_CORE + 4 + r, core_peer))
    for r in range(2, 4):
        new_y[r].wait()
        new_core.append(send_new(1 - s, chunk(h, r), T_NEW_CORE + r, core_peer))
    for copy in grad_core:
        copy.wait()
    for r in range(LINE):
        update(1 - c, chunk(h, r))
        update(1 - c, chunk(1 - h, r))
    m1_out = pltpu.make_async_copy(m1, m1o_hbm, local_sem.at[OUT_M1])
    m1_out.start()
    m2_out = pltpu.make_async_copy(m2, m2o_hbm, local_sem.at[OUT_M2])
    m2_out.start()
    for r in range(2):
        new_x[r].wait()
        new_core.append(send_new(1 - s, chunk(1 - h, r), T_NEW_CORE + 4 + r, core_peer))
    for r in range(2, 4):
        new_y[2 + r].wait()
        new_core.append(send_new(1 - s, chunk(1 - h, r), T_NEW_CORE + 4 + r, core_peer))
    for copy in new_core:
        copy.wait()
    nw_out = []
    for core in range(2):
        target = nw_hbm.at[:, core * cols : (core + 1) * cols]
        copy = pltpu.make_async_copy(nw.at[core], target, local_sem.at[(OUT_W, IN_W)[core]])
        copy.start()
        nw_out.append(copy)
    for copy in ig_out:
        copy.wait()
    m1_out.wait()
    m2_out.wait()
    for copy in nw_out:
        copy.wait()


def hand_over(*refs):
    sources, targets, stages, in_sem, out_sem = refs[:4], refs[4:8], refs[8:12], refs[12], refs[13]
    loads, stores = [], []
    for i, (source, stage) in enumerate(zip(sources, stages)):
        step = source.shape[0] // PIECES
        for j in range(PIECES):
            rows = pl.ds(j * step, step)
            index = i * PIECES + j
            load = pltpu.make_async_copy(source.at[rows], stage.at[rows], in_sem.at[index])
            load.start()
            loads.append(load)
            store = pltpu.make_async_copy(stage.at[rows], targets[i].at[rows], out_sem.at[index])
            stores.append(store)
    for load, store in zip(loads, stores):
        load.wait()
        store.start()
    for store in stores:
        store.wait()


def on_device(
    clips,
    code_grad,
    conv_weight,
    norm_gain,
    proj_weight,
    code_bias,
    rotation,
    first_moment,
    second_moment,
):
    count, frames, sites, width = clips.shape
    bits = code_grad.shape[3]
    dp_size = lax.axis_size("dp")
    devices = dp_size * lax.axis_size("shard")
    far_size = dp_size // DEPTH
    tokens = count * frames * sites
    rows, half = conv_weight.shape[0], first_moment.shape[0]
    per_x, cols = half // 2, width // 2
    own = per_x // LINE
    sizes = (
        count,
        frames,
        sites,
        width,
        bits,
        dp_size,
        far_size,
        tokens * devices,
        count * devices,
    )
    vmem = pltpu.VMEM
    scratch = [
        vmem((tokens, width), BF16),
        vmem((width, tokens), BF16),
        vmem((rows, width), BF16),
        vmem((rows, width), BF16),
        vmem((frames, bits, count, sites), BF16),
        vmem((tokens, width), F32),
        vmem((tokens, 1), F32),
        vmem((BITS_PAD, tokens), F32),
        vmem((BITS_PAD, tokens), F32),
        vmem((128, tokens), F32),
        vmem((128, width), BF16),
        vmem((tokens, width), BF16),
        vmem((tokens, width), BF16),
        vmem((half, width), F32),
        vmem((half, width), F32),
        vmem((rows, cols), F32),
        vmem((rows, cols), BF16),
        vmem((rows, cols), BF16),
        vmem((2, per_x, cols), F32),
        vmem((2, per_x, cols), BF16),
        vmem((2, per_x, cols), BF16),
        vmem((per_x, cols), BF16),
        vmem((per_x, cols), BF16),
        vmem((per_x, cols), BF16),
        vmem((LINE, own, cols), BF16),
        vmem((far_size, own, cols), F32),
        vmem((2, half, cols), BF16),
        vmem((2, rows, cols), BF16),
        vmem((PLANE, BITS_PAD, 128), F32),
        vmem((LINE, BITS_PAD, 128), F32),
        vmem((far_size, BITS_PAD, 128), F32),
        pltpu.SemaphoreType.DMA((IN_X + 2 * count * frames,)),
        pltpu.SemaphoreType.DMA((T_FAR + 2 * far_size,)),
        pltpu.SemaphoreType.DMA((T_FAR + 2 * far_size,)),
    ]
    whole = pl.BlockSpec(memory_space=pltpu.VMEM)
    outside = pl.BlockSpec(memory_space=pl.ANY)
    *large, loss = pl.pallas_call(
        functools.partial(kernel, sizes),
        out_shape=(
            jax.ShapeDtypeStruct((rows, width), BF16),
            jax.ShapeDtypeStruct((half, width), F32),
            jax.ShapeDtypeStruct((half, width), F32),
            jax.ShapeDtypeStruct((tokens, width), BF16),
            jax.ShapeDtypeStruct((1, 1), F32),
        ),
        in_specs=[outside, outside, outside, whole, whole, whole, whole, outside, outside],
        out_specs=(outside, outside, outside, outside, whole),
        scratch_shapes=scratch,
        compiler_params=pltpu.CompilerParams(
            collective_id=0, has_side_effects=True, vmem_limit_bytes=VMEM_BYTES
        ),
    )(
        clips.reshape(tokens, width),
        code_grad.transpose(1, 3, 0, 2),
        conv_weight,
        norm_gain.reshape(1, width),
        proj_weight.T,
        code_bias.reshape(1, bits),
        rotation,
        first_moment,
        second_moment,
    )
    new_weight, first_out, second_out, input_grad = pl.pallas_call(
        hand_over,
        out_shape=tuple(jax.ShapeDtypeStruct(a.shape, a.dtype) for a in large),
        in_specs=[outside] * 4,
        out_specs=(outside,) * 4,
        scratch_shapes=[vmem(a.shape, a.dtype) for a in large]
        + [pltpu.SemaphoreType.DMA((4 * PIECES,))] * 2,
        compiler_params=pltpu.CompilerParams(vmem_limit_bytes=VMEM_BYTES),
    )(*large)
    return (
        new_weight,
        first_out,
        second_out,
        input_grad.reshape(clips.shape),
        loss.reshape(()),
    )


def solution(mesh):
    return jax.shard_map(
        on_device,
        mesh=mesh,
        in_specs=(
            P(("dp", "shard"), None, None, None),
            P(("dp", "shard"), None, None, None),
            P(),
            P(),
            P(),
            P(),
            P(),
            P("shard", None),
            P("shard", None),
        ),
        out_specs=(
            P(),
            P("shard", None),
            P("shard", None),
            P(("dp", "shard"), None, None, None),
            P(),
        ),
        check_vma=False,
    )
```
